128 devices in a mesh: af: 8 (over z, y_hi), sa: 16 (over x, y_lo, core).
Axes of the slice: x: 4, y: 4 (y_hi: 2, y_lo: 2; y = y_hi * 2 + y_lo), z: 4, core: 2. Of those that a mesh axis runs over, the one named last changes fastest.
Arguments:
- tensor: bfloat16 [1024, 1024, 288], P('sa', 'af'), may hold values from -6 to 6
- omega_two: bfloat16 [1024, 256], P('sa'), may hold values from -0.1875 to 0.1875
- omega_three: bfloat16 [288, 256], replicated, may hold values from -0.375 to 0.375
- sketch_rank: bfloat16 [256, 256], P('sa'), may hold values from -0.375 to 0.375
- sketch_plane: bfloat16 [288, 256], replicated, may hold values from -0.375 to 0.375
Outputs:
- core: float32 [256, 256, 288], P('af', 'sa')
The draws below stay inside these ranges and needn't reach their ends.
All inputs are finite; a program needn't handle non-finite values.
Results may differ from the reference program's by a relative error of at most 0.025.
Values may be sent and summed in bfloat16 or wider, within the bound.
No kernel may reach another device: no remote copies, remote signals or barrier semaphores. Data moves between devices by JAX's collectives and lax.ppermute only.
A program may use at most 128 MiB of HBM per device.

```python
import jax
import jax.numpy as jnp
from jax import lax

MODE_ONE = 1024
MODE_TWO = 1024
RANK = 256
PLANES = 288
N_AF = 8
N_SA = 16


def levels(rng, dims, cuts, least, largest):
    loudness = 1.0
    for position, blocks in cuts:
        heights = jax.random.uniform(jax.random.fold_in(jax.random.fold_in(rng, 6), position), (blocks,), jnp.float32, least / len(cuts), largest / len(cuts))
        loudness = loudness * jnp.repeat(jnp.exp(heights), dims[position] // blocks).reshape((-1,) + (1,) * (len(dims) - 1 - position))
    return loudness


def bell_draw(key, extent, spread, reach, split=(), held_as=jnp.bfloat16):
    result = jax.random.normal(key, extent, jnp.float32) * spread
    if len(split) > 0:
        result = levels(key, extent, split, -0.22, 0.18) * result
    return jnp.clip(result, min=-reach, max=reach).astype(held_as)


def setup_inputs(seed: int = 0) -> dict:
    key_of = jax.random.split(jax.random.key(seed), 6)
    return {
        "tensor": bell_draw(key_of[0], (MODE_TWO, MODE_ONE, PLANES), 1.0, 6.0, ((0, 16), (1, 8))),
        "omega_two": bell_draw(key_of[1], (MODE_TWO, RANK), MODE_TWO ** -0.5, 0.1875, ((0, 16),)),
        "omega_three": bell_draw(key_of[2], (PLANES, RANK), PLANES ** -0.5, 0.375),
        "sketch_rank": bell_draw(key_of[3], (RANK, RANK), RANK ** -0.5, 0.375, ((0, 16),)),
        "sketch_plane": bell_draw(key_of[4], (PLANES, RANK), PLANES ** -0.5, 0.375),
    }


HIGH = lax.Precision.HIGHEST

def orthonormal(sketch):
    inner_gram = jnp.dot(sketch.T.astype(jnp.float32), sketch.astype(jnp.float32), precision=HIGH, preferred_element_type=jnp.float32)
    factor = jnp.linalg.cholesky(inner_gram)
    return lax.linalg.triangular_solve(factor, sketch, left_side=False, lower=True, transpose_a=True)

def reference(tensor, omega_two, omega_three, sketch_rank, sketch_plane):
    rows_step = 16
    steps_total = MODE_TWO // rows_step
    tensor_blocks = tensor.reshape(steps_total, rows_step, MODE_ONE, PLANES)
    omega_blocks = omega_two.reshape(steps_total, rows_step, RANK)
    three_wide = omega_three.astype(jnp.float32)

    def sketch_step(running, pieces):
        slab_rows, weights = pieces
        inner = jnp.einsum('jik,kr->jir', slab_rows.astype(jnp.float32), three_wide, precision=HIGH)
        return (running + jnp.einsum('jr,jir->ir', weights.astype(jnp.float32), inner, precision=HIGH), None)
    first_sketch, _ = lax.scan(sketch_step, jnp.zeros((MODE_ONE, RANK), jnp.float32), (tensor_blocks, omega_blocks))
    basis_low = orthonormal(first_sketch).astype(jnp.bfloat16)
    owners = basis_low.astype(jnp.float32).reshape(N_AF, MODE_ONE // N_AF, RANK)

    def project_step(running, slab_rows):
        split_rows = slab_rows.astype(jnp.float32).reshape(rows_step, N_AF, MODE_ONE // N_AF, PLANES)
        terms = jnp.einsum('pia,jpik->jpak', owners, split_rows, precision=HIGH)
        terms = lax.optimization_barrier(terms.astype(jnp.bfloat16)).astype(jnp.float32)
        return (running, jnp.sum(terms, axis=1).astype(jnp.bfloat16))
    _, core_blocks = lax.scan(project_step, jnp.zeros((), jnp.float32), tensor_blocks)
    core_one = core_blocks.reshape(MODE_TWO, RANK, PLANES)
    rank_wide = sketch_rank.astype(jnp.float32)
    plane_wide = sketch_plane.astype(jnp.float32)

    def second_step(running, core_rows):
        inner = jnp.einsum('jak,kr->jar', core_rows.astype(jnp.float32), plane_wide, precision=HIGH)
        return (running, jnp.einsum('ar,jar->jr', rank_wide, inner, precision=HIGH))
    _, second_blocks = lax.scan(second_step, jnp.zeros((), jnp.float32), core_blocks)
    second_sketch = second_blocks.reshape(MODE_TWO, RANK)
    basis_high = orthonormal(second_sketch).astype(jnp.bfloat16)
    fine_rows = MODE_TWO // (N_AF * N_SA)
    core_groups = core_one.reshape(N_SA, N_AF, fine_rows, RANK, PLANES).transpose(1, 0, 2, 3, 4).reshape(N_AF, N_SA * fine_rows, RANK, PLANES)
    basis_groups = basis_high.reshape(N_SA, N_AF, fine_rows, RANK).transpose(1, 0, 2, 3).reshape(N_AF, N_SA * fine_rows, RANK)

    def core_step(running, pieces):
        core_rows, basis_rows = pieces
        terms = jnp.einsum('jc,jak->cak', basis_rows.astype(jnp.float32), core_rows.astype(jnp.float32), precision=HIGH)
        return (running + terms, None)
    total, _ = lax.scan(core_step, jnp.zeros((RANK, RANK, PLANES), jnp.float32), (core_groups, basis_groups))
    return total
```

```python
import jax
import jax.numpy as jnp
from jax import lax
from jax.sharding import PartitionSpec as P

HIGH = lax.Precision.HIGHEST


def orthonormal(sketch):
    gram = jnp.dot(sketch.T, sketch, precision=HIGH, preferred_element_type=jnp.float32)
    factor = jnp.linalg.cholesky(gram)
    return lax.linalg.triangular_solve(
        factor, sketch, left_side=False, lower=True, transpose_a=True
    )


def exchange(blocks, axes):
    return lax.all_to_all(blocks, axes, split_axis=0, concat_axis=0, tiled=True)


def gather(rows, axes, count):
    shared = jnp.broadcast_to(rows[None], (count,) + rows.shape)
    return exchange(shared, axes).reshape(count * rows.shape[0], rows.shape[1])


def on_device(tensor, omega_two, omega_three, sketch_rank, sketch_plane):
    n_af = lax.axis_size("af")
    n_sa = lax.axis_size("sa")
    n_all = n_af * n_sa
    local_rows, local_cols, planes = tensor.shape
    rank = omega_two.shape[1]
    fine_rows = local_rows // n_af
    fine_cols = local_cols // n_sa

    moved = exchange(tensor.reshape(n_af, fine_rows, local_cols, planes), "af")

    inner = jnp.einsum("jik,kr->jir", tensor, omega_three, preferred_element_type=jnp.float32)
    terms = jnp.einsum("jr,jir->ir", omega_two.astype(jnp.float32), inner, precision=HIGH)
    parts = exchange(terms.reshape(n_sa, fine_cols, rank), "sa")
    first_sketch = gather(jnp.sum(parts, axis=0), ("af", "sa"), n_all)
    basis_low = orthonormal(first_sketch).astype(jnp.bfloat16)

    core_one = jnp.einsum(
        "pjik,pia->jak",
        moved,
        basis_low.reshape(n_af, local_cols, rank),
        preferred_element_type=jnp.float32,
    ).astype(jnp.bfloat16)

    plane_inner = jnp.einsum(
        "jak,kr->jar", core_one, sketch_plane, preferred_element_type=jnp.float32
    )
    whole_rank = gather(sketch_rank, "sa", n_sa)
    second_rows = jnp.einsum(
        "ar,jar->jr", whole_rank.astype(jnp.float32), plane_inner, precision=HIGH
    )
    second_sketch = gather(second_rows, ("sa", "af"), n_all)

    share = rank // n_all
    split = core_one.reshape(fine_rows, n_all, share * planes).transpose(1, 0, 2)
    columns = exchange(split, ("sa", "af")).reshape(n_all * fine_rows, share * planes)

    basis_high = orthonormal(second_sketch).astype(jnp.bfloat16)
    core = jnp.dot(basis_high.T, columns, preferred_element_type=jnp.float32)
    swapped = exchange(core.reshape(n_af, rank // n_af, share * planes), "af")
    swapped = swapped.reshape(n_af, rank // n_af, share, planes)
    return swapped.transpose(1, 0, 2, 3).reshape(rank // n_af, n_af * share, planes)


def solution(mesh):
    placed = (P("sa", "af", None), P("sa", None), P(), P("sa", None), P())
    return jax.shard_map(
        on_device, mesh=mesh, in_specs=placed, out_specs=P("af", "sa", None), check_vma=False
    )
```

```python
import jax
import jax.numpy as jnp
from jax import lax
from jax.experimental import pallas as pl
from jax.experimental.pallas import tpu as pltpu
from jax.sharding import Mesh
from jax.sharding import PartitionSpec as P

HIGH = lax.Precision.HIGHEST


NT = (((1,), (1,)), ((), ()))
NN = (((1,), (0,)), ((), ()))
TN = (((0,), (0,)), ((), ()))


def mm(a, b, dims=NN, precision=None):
    return lax.dot_general(a, b, dims, precision=precision, preferred_element_type=jnp.float32)


def low(x):
    return x.astype(jnp.bfloat16)


def inverse_factor(s, basis_ref, a_ref, m_ref):
    n = s.shape[1]
    row = lax.broadcasted_iota(jnp.int32, (n, n), 0)
    col = lax.broadcasted_iota(jnp.int32, (n, n), 1)
    eye = row == col
    one = jnp.where(eye, 1.0, 0.0)
    half = jnp.where(row > col, 1.0, 0.5 * one)
    gram = mm(s, s, TN, HIGH)
    on_diag = jnp.where(eye, gram, 0.0)
    inv_row = 0.9 * lax.rsqrt(jnp.sum(on_diag, axis=0, keepdims=True))
    inv_col = 0.9 * lax.rsqrt(jnp.sum(on_diag, axis=1, keepdims=True))
    scaled = gram * inv_col * inv_row

    h = scaled
    m = None
    early = 2
    for step in range(early):
        f = half * (h - one)
        fb = low(f)
        kb = low(one - f + half * mm(fb, fb, NT) + mm(fb, fb))
        m = kb if m is None else low(mm(kb, m))
        if step < early - 1:
            h = mm(low(mm(kb, low(h))), kb, NT)
    m = m.astype(jnp.float32)
    for _ in range(2):
        r = mm(mm(m, scaled, NN, HIGH), m, NT, HIGH) - one
        m = m - mm(half * r, m, NN, HIGH)
    good = jnp.logical_and(jnp.sum(r * r) < 1e-3, jnp.min(jnp.where(eye, m, 1.0)) > 0.0)
    basis_ref[...] = low(mm(m * inv_row, s, NT, HIGH))

    @pl.when(jnp.logical_not(good))
    def _():
        a_ref[...] = scaled
        m_ref[...] = one

        def step(j, carry):
            a = a_ref[...]
            pivot_row = a_ref[pl.ds(j, 1), :]
            unit_row = m_ref[pl.ds(j, 1), :]
            column = jnp.sum(jnp.where(col == j, a, 0.0), axis=1, keepdims=True)
            pivot = jnp.sum(jnp.where(col[:1] == j, pivot_row, 0.0), axis=1, keepdims=True)
            f = jnp.where(row[:, :1] > j, column / pivot, 0.0)
            a_ref[...] = a - f * pivot_row
            m_ref[...] = m_ref[...] - f * unit_row
            return carry

        lax.fori_loop(0, n, step, 0)
        pivots = jnp.sum(jnp.where(eye, a_ref[...], 0.0), axis=1, keepdims=True)
        direct = m_ref[...] * lax.rsqrt(pivots) * inv_row
        basis_ref[...] = low(mm(direct, s, NT, HIGH))


VMEM = pl.BlockSpec(memory_space=pltpu.VMEM)
PARAMS = pltpu.CompilerParams(vmem_limit_bytes=32 * 1024 * 1024)


def cost(flops, size):
    return pl.CostEstimate(flops=flops, bytes_accessed=size, transcendentals=0)


def first_basis_kernel(s_ref, basis_ref, a_ref, m_ref):
    places = [
        ((c * 2 + yh) * 2 + yl) * 4 + z
        for z in range(4)
        for yh in range(2)
        for c in range(2)
        for yl in range(2)
    ]
    s = jnp.concatenate([s_ref[place * 32 : place * 32 + 32] for place in places], axis=0)
    inverse_factor(s, basis_ref, a_ref, m_ref)


def first_basis(sketch):
    n = sketch.shape[1]
    return pl.pallas_call(
        first_basis_kernel,
        out_shape=jax.ShapeDtypeStruct(sketch.shape[::-1], jnp.bfloat16),
        in_specs=[VMEM],
        out_specs=VMEM,
        scratch_shapes=[pltpu.VMEM((n, n), jnp.float32)] * 2,
        compiler_params=PARAMS,
        cost_estimate=cost(4 * 10**9, 2 * 10**6),
        name="first_basis",
    )(sketch)


def second_core_kernel(got_ref, other_ref, core_ref, basis_ref, a_ref, m_ref):
    lanes = core_ref.shape[1]
    sketch = got_ref[:, lanes:].astype(jnp.float32) + other_ref[...].astype(jnp.float32)
    inverse_factor(sketch, basis_ref, a_ref, m_ref)
    core_ref[...] = mm(basis_ref[...], got_ref[:, :lanes]).astype(core_ref.dtype)


def second_core(got, other):
    n = other.shape[1]
    lanes = got.shape[1] - n
    return pl.pallas_call(
        second_core_kernel,
        out_shape=jax.ShapeDtypeStruct((n, lanes), jnp.bfloat16),
        in_specs=[VMEM] * 2,
        out_specs=VMEM,
        scratch_shapes=[pltpu.VMEM((n, got.shape[0]), jnp.bfloat16)]
        + [pltpu.VMEM((n, n), jnp.float32)] * 2,
        compiler_params=PARAMS,
        cost_estimate=cost(4 * 10**9, 3 * 10**6),
        name="second_core",
    )(got, other)


def project_kernel(basis_ref, plane_ref, rank_ref, moved_ref, split_ref, core_ref):
    count, rows, planes, _ = moved_ref.shape
    rank = basis_ref.shape[0]
    basis = basis_ref[...]
    weight = rank_ref[...].astype(jnp.float32)
    sketch = []
    for j in range(rows):
        slab = jnp.concatenate([moved_ref[b, j] for b in range(count)], axis=1)
        core = low(mm(basis, slab, NT))
        core_ref[j] = core
        inner = mm(core, plane_ref[...])
        sketch.append(jnp.sum(inner * weight, axis=0, keepdims=True))
    sketch = jnp.concatenate(sketch, axis=0)
    upper = low(sketch)
    lower = low(sketch - upper.astype(jnp.float32))
    copies = 64 // rows
    halves = jnp.concatenate([upper] * copies + [lower] * copies, axis=0)

    group = 256 // rows
    pairs = group // 2
    target = lax.broadcasted_iota(jnp.int32, (256, 256), 0)
    source = lax.broadcasted_iota(jnp.int32, (256, 256), 1)
    wanted = (target % rows) * group + 2 * ((target // rows) % pairs) + target // (rows * pairs)
    permute = low(jnp.where(source == wanted, 1.0, 0.0))
    full = planes // 128 * 128
    for g in range(rank // group):
        mixed = jnp.concatenate([core_ref[j, g * group : (g + 1) * group] for j in range(rows)], 0)
        moved = low(mm(permute, mixed))
        even, odd = moved[:128], moved[128:]
        split_ref[g * 128 : (g + 1) * 128] = jnp.concatenate(
            [
                even[:, :full],
                odd[:, :full],
                even[:, full:],
                odd[:, full:],
                jnp.zeros((128, 128 - 2 * (planes - full)), jnp.bfloat16),
                halves,
            ],
            axis=1,
        )


def project(basis, sketch_plane, sketch_rank, moved):
    rows, planes = moved.shape[1:3]
    rank = basis.shape[0]
    lanes = 2 * (planes // 128) * 128 + 128
    return pl.pallas_call(
        project_kernel,
        out_shape=jax.ShapeDtypeStruct((rank // 2 * rows, lanes + rank), jnp.bfloat16),
        in_specs=[VMEM] * 4,
        out_specs=VMEM,
        scratch_shapes=[pltpu.VMEM((rows, rank, planes), jnp.bfloat16)],
        compiler_params=PARAMS,
        cost_estimate=cost(2 * 10**9, 8 * 10**6),
        name="project",
    )(basis, sketch_plane, sketch_rank, moved)


def exchange(blocks, axes):
    return lax.all_to_all(blocks, axes, split_axis=0, concat_axis=0, tiled=True)


def around(block, axes, step):
    count = lax.axis_size(axes)
    return lax.ppermute(block, axes, [(p, (p + step) % count) for p in range(count)])


def ordered(blocks, place):
    count = len(blocks)
    turned = jnp.stack(blocks[::-1] * 2)
    return lax.dynamic_slice_in_dim(turned, count - 1 - place, count, 0)


def collect(block, axes):
    count = lax.axis_size(axes)
    blocks = [block] + [around(block, axes, step) for step in range(1, count)]
    every = ordered(blocks, lax.axis_index(axes))
    return every.reshape((-1,) + block.shape[1:])


def reduce_rows(rows, extra, axes):
    count, me = lax.axis_size(axes), lax.axis_index(axes)
    shares = rows.reshape((count, -1) + rows.shape[1:])
    size = shares.shape[1]
    total = lax.dynamic_index_in_dim(shares, me, 0, keepdims=False)
    extras = [extra]
    for step in range(1, count):
        share = lax.dynamic_index_in_dim(shares, (me + step) % count, 0, keepdims=False)
        got = around(jnp.concatenate([share, extra], axis=0), axes, step)
        total = total + got[:size]
        extras.append(got[size:])
    return total, ordered(extras, me).reshape((-1,) + extra.shape[1:])


AF = ("z", "yh")
SA = ("x", "yl", "c")


def on_device(tensor, omega_two, omega_three, sketch_rank, sketch_plane):
    n_af = lax.axis_size(AF)
    n_sa = lax.axis_size(SA)
    n_all = n_af * n_sa
    local_rows, local_cols, planes = tensor.shape
    rank = omega_two.shape[1]
    fine_rows = local_rows // n_af

    inner = jnp.einsum("jik,kr->jir", tensor, omega_three, preferred_element_type=jnp.float32)
    rows = jnp.einsum("jr,jir->ir", omega_two.astype(jnp.float32), inner, precision=HIGH)
    extra = sketch_rank.astype(jnp.float32)
    for axis in ("c", "yl"):
        rows, extra = reduce_rows(rows, extra, axis)

    rows, tensor = lax.optimization_barrier((rows, tensor))
    pieces = jnp.swapaxes(tensor, 1, 2).reshape(n_af, fine_rows, planes, local_cols)
    moved = exchange(pieces, AF)
    rows, extra = reduce_rows(rows, extra, "x")
    whole_rank = extra.reshape(rank, rank)
    rows = collect(collect(rows, "x"), "z")
    rows, moved = lax.optimization_barrier((rows, moved))
    rows = collect(collect(rows, ("yh", "yl")), "c")
    basis_low = first_basis(rows)

    split = project(basis_low, sketch_plane, whole_rank, moved)
    got = exchange(split.reshape(n_all, fine_rows, -1), SA + AF).reshape(n_all * fine_rows, -1)
    core = second_core(got, around(got[:, -rank:], "c", 1))

    swapped = exchange(core.reshape(n_af, rank // n_af, -1), AF).astype(jnp.float32)
    full = planes // 128 * 128
    rest = planes - full
    even = jnp.concatenate([swapped[..., :full], swapped[..., 2 * full : 2 * full + rest]], -1)
    odd = jnp.concatenate(
        [swapped[..., full : 2 * full], swapped[..., 2 * full + rest : 2 * planes]], -1
    )
    both = jnp.stack([even, odd], axis=2)
    return both.transpose(1, 0, 2, 3).reshape(rank // n_af, 2 * n_af, planes)


def solution(mesh):
    grid = Mesh(mesh.devices.reshape(4, 2, 4, 2, 2), ("z", "yh", "x", "yl", "c"))
    placed = (P(SA, AF, None), P(SA, None), P(), P(SA, None), P())
    return jax.shard_map(
        on_device, mesh=grid, in_specs=placed, out_specs=P(AF, SA, None), check_vma=False
    )
```

```python
import jax
import jax.numpy as jnp
from jax import lax
from jax.experimental import pallas as pl
from jax.experimental.pallas import tpu as pltpu
from jax.sharding import Mesh
from jax.sharding import PartitionSpec as P

HIGH = lax.Precision.HIGHEST


NT = (((1,), (1,)), ((), ()))
NN = (((1,), (0,)), ((), ()))
TN = (((0,), (0,)), ((), ()))


def mm(a, b, dims=NN, precision=None):
    return lax.dot_general(a, b, dims, precision=precision, preferred_element_type=jnp.float32)


def low(x):
    return x.astype(jnp.bfloat16)


def inverse_factor(s, basis_ref, a_ref, m_ref, turned):
    n = s.shape[1]
    row = lax.broadcasted_iota(jnp.int32, (n, n), 0)
    col = lax.broadcasted_iota(jnp.int32, (n, n), 1)
    eye = row == col
    one = jnp.where(eye, 1.0, 0.0)
    half = jnp.where(row > col, 1.0, 0.5 * one)

    def put(inverse):
        basis = mm(inverse, s, NT, HIGH) if turned else mm(s, inverse, NT, HIGH)
        basis_ref[...] = low(basis)

    gram = mm(s, s, TN, HIGH)
    on_diag = jnp.where(eye, gram, 0.0)
    inv_row = 0.9 * lax.rsqrt(jnp.sum(on_diag, axis=0, keepdims=True))
    inv_col = 0.9 * lax.rsqrt(jnp.sum(on_diag, axis=1, keepdims=True))
    scaled = gram * inv_col * inv_row

    h = scaled
    m = None
    early = 2
    for step in range(early):
        f = half * (h - one)
        fb = low(f)
        kb = low(one - f + half * mm(fb, fb, NT) + mm(fb, fb))
        m = kb if m is None else low(mm(kb, m))
        if step < early - 1:
            h = mm(low(mm(kb, low(h))), kb, NT)
    m = m.astype(jnp.float32)
    for _ in range(2):
        r = mm(mm(m, scaled, NN, HIGH), m, NT, HIGH) - one
        m = m - mm(half * r, m, NN, HIGH)
    good = jnp.logical_and(jnp.sum(r * r) < 1e-3, jnp.min(jnp.where(eye, m, 1.0)) > 0.0)
    put(m * inv_row)

    @pl.when(jnp.logical_not(good))
    def _():
        a_ref[...] = scaled
        m_ref[...] = one

        def step(j, carry):
            a = a_ref[...]
            pivot_row = a_ref[pl.ds(j, 1), :]
            unit_row = m_ref[pl.ds(j, 1), :]
            column = jnp.sum(jnp.where(col == j, a, 0.0), axis=1, keepdims=True)
            pivot = jnp.sum(jnp.where(col[:1] == j, pivot_row, 0.0), axis=1, keepdims=True)
            f = jnp.where(row[:, :1] > j, column / pivot, 0.0)
            a_ref[...] = a - f * pivot_row
            m_ref[...] = m_ref[...] - f * unit_row
            return carry

        lax.fori_loop(0, n, step, 0)
        pivots = jnp.sum(jnp.where(eye, a_ref[...], 0.0), axis=1, keepdims=True)
        direct = m_ref[...] * lax.rsqrt(pivots) * inv_row
        put(direct)


VMEM = pl.BlockSpec(memory_space=pltpu.VMEM)
PARAMS = pltpu.CompilerParams(vmem_limit_bytes=32 * 1024 * 1024)
ROOMY = pltpu.CompilerParams(vmem_limit_bytes=60 * 1024 * 1024)


def cost(flops, size):
    return pl.CostEstimate(flops=flops, bytes_accessed=size, transcendentals=0)


def first_basis_kernel(s_ref, basis_ref, a_ref, m_ref):
    places = [
        ((c * 4 + z) * 2 + yh) * 2 + yl
        for z in range(4)
        for yh in range(2)
        for yl in range(2)
        for c in range(2)
    ]
    s = jnp.concatenate([s_ref[place * 32 : place * 32 + 32] for place in places], axis=0)
    inverse_factor(s, basis_ref, a_ref, m_ref, False)


def first_basis(sketch):
    n = sketch.shape[1]
    return pl.pallas_call(
        first_basis_kernel,
        out_shape=jax.ShapeDtypeStruct(sketch.shape, jnp.bfloat16),
        in_specs=[VMEM],
        out_specs=VMEM,
        scratch_shapes=[pltpu.VMEM((n, n), jnp.float32)] * 2,
        compiler_params=PARAMS,
        cost_estimate=cost(0, 0),
        name="first_basis",
    )(sketch)


def second_core_kernel(got_ref, other_ref, core_ref, basis_ref, a_ref, m_ref):
    lanes = core_ref.shape[1]
    sketch = got_ref[:, lanes:].astype(jnp.float32) + other_ref[...].astype(jnp.float32)
    inverse_factor(sketch, basis_ref, a_ref, m_ref, True)
    core_ref[...] = mm(basis_ref[...], got_ref[:, :lanes]).astype(core_ref.dtype)


def second_core(got, other):
    n = other.shape[1]
    lanes = got.shape[1] - n
    return pl.pallas_call(
        second_core_kernel,
        out_shape=jax.ShapeDtypeStruct((n, lanes), jnp.bfloat16),
        in_specs=[VMEM] * 2,
        out_specs=VMEM,
        scratch_shapes=[pltpu.VMEM((n, got.shape[0]), jnp.bfloat16)]
        + [pltpu.VMEM((n, n), jnp.float32)] * 2,
        compiler_params=PARAMS,
        cost_estimate=cost(4 * 10**9, 3 * 10**6),
        name="second_core",
    )(got, other)


def first_sums_kernel(two_ref, three_ref, slabs_ref, out_ref):
    step = pl.program_id(0)
    count = slabs_ref.shape[0]
    weight = two_ref[pl.ds(pl.multiple_of(step * count, count), count), :]
    weight = weight.astype(jnp.float32)
    total = None
    for j in range(count):
        inner = mm(slabs_ref[j], three_ref[...], TN)
        term = inner * weight[j : j + 1]
        total = term if total is None else total + term

    @pl.when(step == 0)
    def _():
        out_ref[...] = total

    @pl.when(step > 0)
    def _():
        out_ref[...] += total


def first_sums(tensor, omega_two, omega_three):
    rows, cols, planes = tensor.shape
    rank = omega_two.shape[1]
    count = 16
    return pl.pallas_call(
        first_sums_kernel,
        grid=(rows // count,),
        out_shape=jax.ShapeDtypeStruct((cols, rank), jnp.float32),
        in_specs=[
            pl.BlockSpec((rows, rank), lambda step: (0, 0)),
            pl.BlockSpec((planes, rank), lambda step: (0, 0)),
            pl.BlockSpec((count, planes, cols), lambda step: (step, 0, 0)),
        ],
        out_specs=pl.BlockSpec((cols, rank), lambda step: (0, 0)),
        compiler_params=ROOMY,
        cost_estimate=cost(10**9, 5 * 10**6),
        name="first_sums",
    )(omega_two, omega_three, jnp.swapaxes(tensor, 1, 2))


def project_kernel(basis_ref, plane_ref, rank_ref, moved_ref, split_ref, core_ref, slab_ref, sems):
    rows, rank, planes = core_ref.shape
    loads = [
        pltpu.make_async_copy(moved_ref.at[:, j], slab_ref.at[j], sems.at[j]) for j in range(rows)
    ]
    for load in loads:
        load.start()
    basis = basis_ref[...]
    weight = plane_ref[...].astype(jnp.float32)
    sketch = []
    for j in range(rows):
        loads[j].wait()
        slab = jnp.concatenate([slab_ref[j, b] for b in range(slab_ref.shape[1])], axis=1)
        core = mm(slab, basis)
        core_ref[j] = low(core.T)
        inner = mm(low(core), rank_ref[...])
        sketch.append(jnp.sum(inner * weight, axis=0, keepdims=True))
    sketch = jnp.concatenate(sketch, axis=0)
    upper = low(sketch)
    lower = low(sketch - upper.astype(jnp.float32))
    copies = 64 // rows
    halves = jnp.concatenate([upper] * copies + [lower] * copies, axis=0)

    group = 256 // rows
    pairs = group // 2
    target = lax.broadcasted_iota(jnp.int32, (256, 256), 0)
    source = lax.broadcasted_iota(jnp.int32, (256, 256), 1)
    wanted = (target % rows) * group + 2 * ((target // rows) % pairs) + target // (rows * pairs)
    permute = low(jnp.where(source == wanted, 1.0, 0.0))
    full = planes // 128 * 128
    gap = jnp.zeros((128, 128 - 2 * (planes - full)), jnp.bfloat16)
    for g in range(rank // group):
        mixed = [core_ref[j, g * group : (g + 1) * group] for j in range(rows)]
        sorted_rows = low(mm(permute, jnp.concatenate(mixed, axis=0)))
        even, odd = sorted_rows[:128], sorted_rows[128:]
        split_ref[g * 128 : (g + 1) * 128] = jnp.concatenate(
            [even[:, :full], odd[:, :full], even[:, full:], odd[:, full:], gap, halves], axis=1
        )


def project(basis, sketch_plane, sketch_rank, moved):
    blocks, rows, planes, width = moved.shape
    rank = basis.shape[1]
    lanes = 2 * (planes // 128) * 128 + 128
    return pl.pallas_call(
        project_kernel,
        out_shape=jax.ShapeDtypeStruct((rank // 2 * rows, lanes + rank), jnp.bfloat16),
        in_specs=[VMEM] * 3 + [pl.BlockSpec(memory_space=pl.ANY)],
        out_specs=VMEM,
        scratch_shapes=[
            pltpu.VMEM((rows, rank, planes), jnp.bfloat16),
            pltpu.VMEM((rows, blocks, planes, width), jnp.bfloat16),
            pltpu.SemaphoreType.DMA((rows,)),
        ],
        compiler_params=PARAMS,
        cost_estimate=cost(2 * 10**9, 8 * 10**6),
        name="project",
    )(basis, sketch_plane, sketch_rank, moved)


def merge_kernel(got_ref, out_ref):
    blocks, count, _ = got_ref.shape
    planes = out_ref.shape[2]
    full = planes // 128 * 128
    rest = planes - full
    group = 256 // (2 * blocks)
    target = lax.broadcasted_iota(jnp.int32, (256, 256), 0)
    source = lax.broadcasted_iota(jnp.int32, (256, 256), 1)
    wanted = (target % (2 * blocks)) * group + target // (2 * blocks)
    permute = low(jnp.where(source == wanted, 1.0, 0.0))
    for g in range(count // group):
        rows = []
        for b in range(blocks):
            got = got_ref[b, g * group : (g + 1) * group]
            tail = 2 * full
            rows.append(jnp.concatenate([got[:, :full], got[:, tail : tail + rest]], axis=1))
            rows.append(
                jnp.concatenate([got[:, full:tail], got[:, tail + rest : tail + 2 * rest]], axis=1)
            )
        moved = mm(permute, jnp.concatenate(rows, axis=0))
        out_ref[g * group : (g + 1) * group] = moved.reshape(group, 2 * blocks, planes)


def merge(got, planes):
    return pl.pallas_call(
        merge_kernel,
        out_shape=jax.ShapeDtypeStruct((got.shape[1], 2 * got.shape[0], planes), jnp.float32),
        in_specs=[VMEM],
        out_specs=VMEM,
        compiler_params=PARAMS,
        cost_estimate=cost(10**8, 10**6),
        name="merge",
    )(got)


def exchange(blocks, axes):
    return lax.all_to_all(blocks, axes, split_axis=0, concat_axis=0, tiled=True)


def gather(rows, axes, count):
    shared = jnp.broadcast_to(rows[None], (count,) + rows.shape)
    return exchange(shared, axes).reshape(count * rows.shape[0], rows.shape[1])


def around(block, axes, step):
    count = lax.axis_size(axes)
    return lax.ppermute(block, axes, [(p, (p + step) % count) for p in range(count)])


def ordered(blocks, place):
    count = len(blocks)
    turned = jnp.stack(blocks[::-1] * 2)
    return lax.dynamic_slice_in_dim(turned, count - 1 - place, count, 0)


def collect(block, axes):
    count = lax.axis_size(axes)
    blocks = [block] + [around(block, axes, step) for step in range(1, count)]
    every = ordered(blocks, lax.axis_index(axes))
    return every.reshape((-1,) + block.shape[1:])


AF = ("z", "yh")
SA = ("x", "yl", "c")


def on_device(tensor, omega_two, omega_three, sketch_rank, sketch_plane):
    n_af = lax.axis_size(AF)
    n_sa = lax.axis_size(SA)
    n_all = n_af * n_sa
    local_rows, local_cols, planes = tensor.shape
    rank = omega_two.shape[1]
    fine_rows = local_rows // n_af

    rows = first_sums(tensor, omega_two, omega_three)
    some_rank = collect(sketch_rank, "yl")

    parts = exchange(rows.reshape(4, -1, rank), ("yl", "c"))
    rows, some_rank = lax.optimization_barrier((jnp.sum(parts, axis=0), some_rank))
    rows = gather(rows, AF + ("yl",), n_af * 2)

    rows, tensor = lax.optimization_barrier((rows, tensor))
    pieces = jnp.swapaxes(tensor, 1, 2).reshape(n_af, fine_rows, planes, local_cols)
    moved = exchange(pieces, AF)

    n_x, at = lax.axis_size("x"), lax.axis_index("x")
    shares = rows.reshape(n_x, -1, rank)
    rows = lax.dynamic_index_in_dim(shares, at, 0, keepdims=False)
    for step in range(1, n_x):
        share = lax.dynamic_index_in_dim(shares, (at + step) % n_x, 0, keepdims=False)
        rows = rows + around(share, "x", step)
    rows = collect(collect(rows, "x"), "c")
    whole_rank = collect(collect(some_rank, "c"), "x").reshape(4, 2, 2, -1, rank)
    whole_rank = whole_rank.swapaxes(1, 2).reshape(rank, rank)
    basis_low = first_basis(rows)

    split = project(basis_low, sketch_plane, whole_rank, moved)
    got = exchange(split.reshape(n_all, fine_rows, -1), SA + AF).reshape(n_all * fine_rows, -1)
    core = second_core(got, around(got[:, -rank:], "c", 1))

    return merge(exchange(core.reshape(n_af, rank // n_af, -1), AF), planes)


def solution(mesh):
    grid = Mesh(mesh.devices.reshape(4, 2, 4, 2, 2), ("z", "yh", "x", "yl", "c"))
    placed = (P(SA, AF, None), P(SA, None), P(), P(SA, None), P())
    return jax.shard_map(
        on_device, mesh=grid, in_specs=placed, out_specs=P(AF, SA, None), check_vma=False
    )
```

```python
import jax
import jax.numpy as jnp
from jax import lax
from jax.experimental import pallas as pl
from jax.experimental.pallas import tpu as pltpu
from jax.sharding import Mesh
from jax.sharding import PartitionSpec as P

HIGH = lax.Precision.HIGHEST


NT = (((1,), (1,)), ((), ()))
NN = (((1,), (0,)), ((), ()))
TN = (((0,), (0,)), ((), ()))


def mm(a, b, dims=NN, precision=None):
    return lax.dot_general(a, b, dims, precision=precision, preferred_element_type=jnp.float32)


def low(x):
    return x.astype(jnp.bfloat16)


def inverse_factor(s, basis_ref, a_ref, m_ref, turned):
    n = s.shape[1]
    row = lax.broadcasted_iota(jnp.int32, (n, n), 0)
    col = lax.broadcasted_iota(jnp.int32, (n, n), 1)
    eye = row == col
    one = jnp.where(eye, 1.0, 0.0)
    half = jnp.where(row > col, 1.0, 0.5 * one)

    def put(inverse):
        basis = mm(inverse, s, NT, HIGH) if turned else mm(s, inverse, NT, HIGH)
        basis_ref[...] = low(basis)

    gram = mm(s, s, TN, HIGH)
    on_diag = jnp.where(eye, gram, 0.0)
    inv_row = 0.9 * lax.rsqrt(jnp.sum(on_diag, axis=0, keepdims=True))
    inv_col = 0.9 * lax.rsqrt(jnp.sum(on_diag, axis=1, keepdims=True))
    scaled = gram * inv_col * inv_row

    h = scaled
    m = None
    early = 2
    for step in range(early):
        f = half * (h - one)
        fb = low(f)
        kb = low(one - f + half * mm(fb, fb, NT) + mm(fb, fb))
        m = kb if m is None else low(mm(kb, m))
        if step < early - 1:
            h = mm(low(mm(kb, low(h))), kb, NT)
    m = m.astype(jnp.float32)
    for _ in range(2):
        r = mm(mm(m, scaled, NN, HIGH), m, NT, HIGH) - one
        m = m - mm(half * r, m, NN, HIGH)
    good = jnp.logical_and(jnp.sum(r * r) < 1e-3, jnp.min(jnp.where(eye, m, 1.0)) > 0.0)
    put(m * inv_row)

    @pl.when(jnp.logical_not(good))
    def _():
        a_ref[...] = scaled
        m_ref[...] = one

        def step(j, carry):
            a = a_ref[...]
            pivot_row = a_ref[pl.ds(j, 1), :]
            unit_row = m_ref[pl.ds(j, 1), :]
            column = jnp.sum(jnp.where(col == j, a, 0.0), axis=1, keepdims=True)
            pivot = jnp.sum(jnp.where(col[:1] == j, pivot_row, 0.0), axis=1, keepdims=True)
            f = jnp.where(row[:, :1] > j, column / pivot, 0.0)
            a_ref[...] = a - f * pivot_row
            m_ref[...] = m_ref[...] - f * unit_row
            return carry

        lax.fori_loop(0, n, step, 0)
        pivots = jnp.sum(jnp.where(eye, a_ref[...], 0.0), axis=1, keepdims=True)
        direct = m_ref[...] * lax.rsqrt(pivots) * inv_row
        put(direct)


VMEM = pl.BlockSpec(memory_space=pltpu.VMEM)
PARAMS = pltpu.CompilerParams(vmem_limit_bytes=32 * 1024 * 1024)
ROOMY = pltpu.CompilerParams(vmem_limit_bytes=60 * 1024 * 1024)


def cost(flops, size):
    return pl.CostEstimate(flops=flops, bytes_accessed=size, transcendentals=0)


def first_basis_kernel(s_ref, basis_ref, a_ref, m_ref):
    places = [
        (((c * 4 + x) * 4 + z) * 2 + yh) * 2 + yl
        for z in range(4)
        for yh in range(2)
        for x in range(4)
        for yl in range(2)
        for c in range(2)
    ]
    s = jnp.concatenate([s_ref[place * 8 : place * 8 + 8] for place in places], axis=0)
    inverse_factor(s, basis_ref, a_ref, m_ref, False)


def first_basis(sketch):
    n = sketch.shape[1]
    return pl.pallas_call(
        first_basis_kernel,
        out_shape=jax.ShapeDtypeStruct(sketch.shape, jnp.bfloat16),
        in_specs=[VMEM],
        out_specs=VMEM,
        scratch_shapes=[pltpu.VMEM((n, n), jnp.float32)] * 2,
        compiler_params=PARAMS,
        cost_estimate=cost(0, 0),
        name="first_basis",
    )(sketch)


def second_core_kernel(got_ref, other_ref, core_ref, basis_ref, a_ref, m_ref):
    lanes = core_ref.shape[1]
    sketch = got_ref[:, lanes:].astype(jnp.float32) + other_ref[...].astype(jnp.float32)
    inverse_factor(sketch, basis_ref, a_ref, m_ref, True)
    core_ref[...] = mm(basis_ref[...], got_ref[:, :lanes]).astype(core_ref.dtype)


def second_core(got, other):
    n = other.shape[1]
    lanes = got.shape[1] - n
    return pl.pallas_call(
        second_core_kernel,
        out_shape=jax.ShapeDtypeStruct((n, lanes), jnp.bfloat16),
        in_specs=[VMEM] * 2,
        out_specs=VMEM,
        scratch_shapes=[pltpu.VMEM((n, got.shape[0]), jnp.bfloat16)]
        + [pltpu.VMEM((n, n), jnp.float32)] * 2,
        compiler_params=PARAMS,
        cost_estimate=cost(4 * 10**9, 3 * 10**6),
        name="second_core",
    )(got, other)


def first_sums_kernel(two_ref, three_ref, slabs_ref, out_ref):
    step = pl.program_id(0)
    count = slabs_ref.shape[0]
    weight = two_ref[pl.ds(pl.multiple_of(step * count, count), count), :]
    weight = weight.astype(jnp.float32)
    total = None
    for j in range(count):
        inner = mm(slabs_ref[j], three_ref[...], TN)
        term = inner * weight[j : j + 1]
        total = term if total is None else total + term

    @pl.when(step == 0)
    def _():
        out_ref[...] = total

    @pl.when(step > 0)
    def _():
        out_ref[...] += total


def first_sums(tensor, omega_two, omega_three):
    rows, cols, planes = tensor.shape
    rank = omega_two.shape[1]
    count = 16
    return pl.pallas_call(
        first_sums_kernel,
        grid=(rows // count,),
        out_shape=jax.ShapeDtypeStruct((cols, rank), jnp.float32),
        in_specs=[
            pl.BlockSpec((rows, rank), lambda step: (0, 0)),
            pl.BlockSpec((planes, rank), lambda step: (0, 0)),
            pl.BlockSpec((count, planes, cols), lambda step: (step, 0, 0)),
        ],
        out_specs=pl.BlockSpec((cols, rank), lambda step: (0, 0)),
        compiler_params=ROOMY,
        cost_estimate=cost(10**9, 5 * 10**6),
        name="first_sums",
    )(omega_two, omega_three, jnp.swapaxes(tensor, 1, 2))


def project_kernel(basis_ref, plane_ref, rank_ref, moved_ref, split_ref, core_ref, slab_ref, sems):
    rows, rank, planes = core_ref.shape
    loads = [
        pltpu.make_async_copy(moved_ref.at[:, j], slab_ref.at[j], sems.at[j]) for j in range(rows)
    ]
    for load in loads:
        load.start()
    basis = basis_ref[...]
    weight = plane_ref[...].astype(jnp.float32)
    sketch = []
    for j in range(rows):
        loads[j].wait()
        slab = jnp.concatenate([slab_ref[j, b] for b in range(slab_ref.shape[1])], axis=1)
        core = mm(slab, basis)
        core_ref[j] = low(core.T)
        inner = mm(low(core), rank_ref[...])
        sketch.append(jnp.sum(inner * weight, axis=0, keepdims=True))
    sketch = jnp.concatenate(sketch, axis=0)
    upper = low(sketch)
    lower = low(sketch - upper.astype(jnp.float32))
    copies = 64 // rows
    halves = jnp.concatenate([upper] * copies + [lower] * copies, axis=0)

    group = 256 // rows
    pairs = group // 2
    target = lax.broadcasted_iota(jnp.int32, (256, 256), 0)
    source = lax.broadcasted_iota(jnp.int32, (256, 256), 1)
    wanted = (target % rows) * group + 2 * ((target // rows) % pairs) + target // (rows * pairs)
    permute = low(jnp.where(source == wanted, 1.0, 0.0))
    full = planes // 128 * 128
    gap = jnp.zeros((128, 128 - 2 * (planes - full)), jnp.bfloat16)
    for g in range(rank // group):
        mixed = [core_ref[j, g * group : (g + 1) * group] for j in range(rows)]
        sorted_rows = low(mm(permute, jnp.concatenate(mixed, axis=0)))
        even, odd = sorted_rows[:128], sorted_rows[128:]
        split_ref[g * 128 : (g + 1) * 128] = jnp.concatenate(
            [even[:, :full], odd[:, :full], even[:, full:], odd[:, full:], gap, halves], axis=1
        )


def project(basis, sketch_plane, sketch_rank, moved):
    blocks, rows, planes, width = moved.shape
    rank = basis.shape[1]
    lanes = 2 * (planes // 128) * 128 + 128
    return pl.pallas_call(
        project_kernel,
        out_shape=jax.ShapeDtypeStruct((rank // 2 * rows, lanes + rank), jnp.bfloat16),
        in_specs=[VMEM] * 3 + [pl.BlockSpec(memory_space=pl.ANY)],
        out_specs=VMEM,
        scratch_shapes=[
            pltpu.VMEM((rows, rank, planes), jnp.bfloat16),
            pltpu.VMEM((rows, blocks, planes, width), jnp.bfloat16),
            pltpu.SemaphoreType.DMA((rows,)),
        ],
        compiler_params=PARAMS,
        cost_estimate=cost(2 * 10**9, 8 * 10**6),
        name="project",
    )(basis, sketch_plane, sketch_rank, moved)


def merge_kernel(got_ref, out_ref):
    blocks, count, _ = got_ref.shape
    planes = out_ref.shape[2]
    full = planes // 128 * 128
    rest = planes - full
    group = 256 // (2 * blocks)
    target = lax.broadcasted_iota(jnp.int32, (256, 256), 0)
    source = lax.broadcasted_iota(jnp.int32, (256, 256), 1)
    wanted = (target % (2 * blocks)) * group + target // (2 * blocks)
    permute = low(jnp.where(source == wanted, 1.0, 0.0))
    for g in range(count // group):
        rows = []
        for b in range(blocks):
            got = got_ref[b, g * group : (g + 1) * group]
            tail = 2 * full
            rows.append(jnp.concatenate([got[:, :full], got[:, tail : tail + rest]], axis=1))
            rows.append(
                jnp.concatenate([got[:, full:tail], got[:, tail + rest : tail + 2 * rest]], axis=1)
            )
        moved = mm(permute, jnp.concatenate(rows, axis=0))
        out_ref[g * group : (g + 1) * group] = moved.reshape(group, 2 * blocks, planes)


def merge(got, planes):
    return pl.pallas_call(
        merge_kernel,
        out_shape=jax.ShapeDtypeStruct((got.shape[1], 2 * got.shape[0], planes), jnp.float32),
        in_specs=[VMEM],
        out_specs=VMEM,
        compiler_params=PARAMS,
        cost_estimate=cost(10**8, 10**6),
        name="merge",
    )(got)


def exchange(blocks, axes):
    return lax.all_to_all(blocks, axes, split_axis=0, concat_axis=0, tiled=True)


def gather(rows, axes, count):
    shared = jnp.broadcast_to(rows[None], (count,) + rows.shape)
    return exchange(shared, axes).reshape(count * rows.shape[0], rows.shape[1])


def around(block, axes, step):
    count = lax.axis_size(axes)
    return lax.ppermute(block, axes, [(p, (p + step) % count) for p in range(count)])


def ordered(blocks, place):
    count = len(blocks)
    turned = jnp.stack(blocks[::-1] * 2)
    return lax.dynamic_slice_in_dim(turned, count - 1 - place, count, 0)


def collect(block, axes):
    count = lax.axis_size(axes)
    blocks = [block] + [around(block, axes, step) for step in range(1, count)]
    every = ordered(blocks, lax.axis_index(axes))
    return every.reshape((-1,) + block.shape[1:])


AF = ("z", "yh")
SA = ("x", "yl", "c")


def on_device(tensor, omega_two, omega_three, sketch_rank, sketch_plane):
    n_af = lax.axis_size(AF)
    n_sa = lax.axis_size(SA)
    n_all = n_af * n_sa
    local_rows, local_cols, planes = tensor.shape
    rank = omega_two.shape[1]
    fine_rows = local_rows // n_af

    rows = first_sums(tensor, omega_two, omega_three)
    some_rank = collect(sketch_rank, "yl")

    parts = exchange(rows.reshape(n_sa, -1, rank), SA)
    rows, some_rank = lax.optimization_barrier((jnp.sum(parts, axis=0), some_rank))
    rows = gather(rows, AF + ("yl",), n_af * 2)

    rows, tensor = lax.optimization_barrier((rows, tensor))
    pieces = jnp.swapaxes(tensor, 1, 2).reshape(n_af, fine_rows, planes, local_cols)
    moved = exchange(pieces, AF)

    rows = collect(collect(rows, "x"), "c")
    whole_rank = collect(collect(some_rank, "c"), "x").reshape(4, 2, 2, -1, rank)
    whole_rank = whole_rank.swapaxes(1, 2).reshape(rank, rank)
    basis_low = first_basis(rows)

    split = project(basis_low, sketch_plane, whole_rank, moved)
    got = exchange(split.reshape(n_all, fine_rows, -1), SA + AF).reshape(n_all * fine_rows, -1)
    core = second_core(got, around(got[:, -rank:], "c", 1))

    return merge(exchange(core.reshape(n_af, rank // n_af, -1), AF), planes)


def solution(mesh):
    grid = Mesh(mesh.devices.reshape(4, 2, 4, 2, 2), ("z", "yh", "x", "yl", "c"))
    placed = (P(SA, AF, None), P(SA, None), P(), P(SA, None), P())
    return jax.shard_map(
        on_device, mesh=grid, in_specs=placed, out_specs=P(AF, SA, None), check_vma=False
    )
```

```python
import jax
import jax.numpy as jnp
from jax import lax
from jax.experimental import pallas as pl
from jax.experimental.pallas import tpu as pltpu
from jax.sharding import Mesh
from jax.sharding import PartitionSpec as P

HIGH = lax.Precision.HIGHEST


NT = (((1,), (1,)), ((), ()))
NN = (((1,), (0,)), ((), ()))
TN = (((0,), (0,)), ((), ()))


def mm(a, b, dims=NN, precision=None):
    return lax.dot_general(a, b, dims, precision=precision, preferred_element_type=jnp.float32)


def low(x):
    return x.astype(jnp.bfloat16)


def halves_of(x):
    upper = low(x)
    return upper, low(x - upper.astype(jnp.float32))


def fine(a, b, dims=NN):
    return mm(a[0], b[0], dims) + (mm(a[0], b[1], dims) + mm(a[1], b[0], dims))


def inverse_factor(s, basis_ref, a_ref, m_ref, turned):
    n = s.shape[1]
    row = lax.broadcasted_iota(jnp.int32, (n, n), 0)
    col = lax.broadcasted_iota(jnp.int32, (n, n), 1)
    eye = row == col
    one = jnp.where(eye, 1.0, 0.0)
    half = jnp.where(row > col, 1.0, 0.5 * one)

    sketch = halves_of(s)

    def put(inverse):
        inverse = halves_of(inverse)
        basis_ref[...] = low(fine(inverse, sketch, NT) if turned else fine(sketch, inverse, NT))

    gram = mm(s, s, TN, HIGH)
    on_diag = jnp.where(eye, gram, 0.0)
    inv_row = 0.9 * lax.rsqrt(jnp.sum(on_diag, axis=0, keepdims=True))
    inv_col = 0.9 * lax.rsqrt(jnp.sum(on_diag, axis=1, keepdims=True))
    scaled = gram * inv_col * inv_row

    h = scaled
    m = None
    early = 2
    for step in range(early):
        f = half * (h - one)
        fb = low(f)
        kb = low(one - f + half * mm(fb, fb, NT) + mm(fb, fb))
        m = kb if m is None else low(mm(kb, m))
        if step < early - 1:
            h = mm(low(mm(kb, low(h))), kb, NT)
    m = m.astype(jnp.float32)
    gram = halves_of(scaled)
    for _ in range(2):
        both = halves_of(m)
        r = fine(halves_of(fine(both, gram)), both, NT) - one
        m = m - fine(halves_of(half * r), both)
    good = jnp.logical_and(jnp.sum(r * r) < 1e-3, jnp.min(jnp.where(eye, m, 1.0)) > 0.0)
    put(m * inv_row)

    @pl.when(jnp.logical_not(good))
    def _():
        a_ref[...] = scaled
        m_ref[...] = one

        def step(j, carry):
            a = a_ref[...]
            pivot_row = a_ref[pl.ds(j, 1), :]
            unit_row = m_ref[pl.ds(j, 1), :]
            column = jnp.sum(jnp.where(col == j, a, 0.0), axis=1, keepdims=True)
            pivot = jnp.sum(jnp.where(col[:1] == j, pivot_row, 0.0), axis=1, keepdims=True)
            f = jnp.where(row[:, :1] > j, column / pivot, 0.0)
            a_ref[...] = a - f * pivot_row
            m_ref[...] = m_ref[...] - f * unit_row
            return carry

        lax.fori_loop(0, n, step, 0)
        pivots = jnp.sum(jnp.where(eye, a_ref[...], 0.0), axis=1, keepdims=True)
        direct = m_ref[...] * lax.rsqrt(pivots) * inv_row
        put(direct)


VMEM = pl.BlockSpec(memory_space=pltpu.VMEM)
PARAMS = pltpu.CompilerParams(vmem_limit_bytes=32 * 1024 * 1024)
ROOMY = pltpu.CompilerParams(vmem_limit_bytes=60 * 1024 * 1024)


def cost(flops, size):
    return pl.CostEstimate(flops=flops, bytes_accessed=size, transcendentals=0)


def first_basis_kernel(s_ref, basis_ref, a_ref, m_ref):
    places = [
        (((c * 4 + x) * 4 + z) * 2 + yh) * 2 + yl
        for z in range(4)
        for yh in range(2)
        for x in range(4)
        for yl in range(2)
        for c in range(2)
    ]
    s = jnp.concatenate([s_ref[place * 8 : place * 8 + 8] for place in places], axis=0)
    inverse_factor(s, basis_ref, a_ref, m_ref, False)


def first_basis(sketch):
    n = sketch.shape[1]
    return pl.pallas_call(
        first_basis_kernel,
        out_shape=jax.ShapeDtypeStruct(sketch.shape, jnp.bfloat16),
        in_specs=[VMEM],
        out_specs=VMEM,
        scratch_shapes=[pltpu.VMEM((n, n), jnp.float32)] * 2,
        compiler_params=PARAMS,
        cost_estimate=cost(0, 0),
        name="first_basis",
    )(sketch)


def second_core_kernel(got_ref, other_ref, core_ref, basis_ref, a_ref, m_ref):
    lanes = core_ref.shape[1]
    sketch = got_ref[:, lanes:].astype(jnp.float32) + other_ref[...].astype(jnp.float32)
    inverse_factor(sketch, basis_ref, a_ref, m_ref, True)
    core_ref[...] = mm(basis_ref[...], got_ref[:, :lanes]).astype(core_ref.dtype)


def second_core(got, other):
    n = other.shape[1]
    lanes = got.shape[1] - n
    return pl.pallas_call(
        second_core_kernel,
        out_shape=jax.ShapeDtypeStruct((n, lanes), jnp.bfloat16),
        in_specs=[VMEM] * 2,
        out_specs=VMEM,
        scratch_shapes=[pltpu.VMEM((n, got.shape[0]), jnp.bfloat16)]
        + [pltpu.VMEM((n, n), jnp.float32)] * 2,
        compiler_params=PARAMS,
        cost_estimate=cost(4 * 10**9, 3 * 10**6),
        name="second_core",
    )(got, other)


def first_sums_kernel(two_ref, three_ref, slabs_ref, out_ref):
    step = pl.program_id(0)
    count = slabs_ref.shape[0]
    weight = two_ref[pl.ds(pl.multiple_of(step * count, count), count), :]
    weight = weight.astype(jnp.float32)
    total = None
    for j in range(count):
        inner = mm(slabs_ref[j], three_ref[...], TN)
        term = inner * weight[j : j + 1]
        total = term if total is None else total + term

    @pl.when(step == 0)
    def _():
        out_ref[...] = total

    @pl.when(step > 0)
    def _():
        out_ref[...] += total


def first_sums(tensor, omega_two, omega_three):
    rows, cols, planes = tensor.shape
    rank = omega_two.shape[1]
    count = 16
    return pl.pallas_call(
        first_sums_kernel,
        grid=(rows // count,),
        out_shape=jax.ShapeDtypeStruct((cols, rank), jnp.float32),
        in_specs=[
            pl.BlockSpec((rows, rank), lambda step: (0, 0)),
            pl.BlockSpec((planes, rank), lambda step: (0, 0)),
            pl.BlockSpec((count, planes, cols), lambda step: (step, 0, 0)),
        ],
        out_specs=pl.BlockSpec((cols, rank), lambda step: (0, 0)),
        compiler_params=ROOMY,
        cost_estimate=cost(10**9, 5 * 10**6),
        name="first_sums",
    )(omega_two, omega_three, jnp.swapaxes(tensor, 1, 2))


def project_kernel(basis_ref, plane_ref, rank_ref, moved_ref, split_ref, core_ref, slab_ref, sems):
    rows, rank, planes = core_ref.shape
    loads = [
        pltpu.make_async_copy(moved_ref.at[:, j], slab_ref.at[j], sems.at[j]) for j in range(rows)
    ]
    for load in loads:
        load.start()
    basis = basis_ref[...]
    weight = plane_ref[...].astype(jnp.float32)
    sketch = []
    for j in range(rows):
        loads[j].wait()
        slab = jnp.concatenate([slab_ref[j, b] for b in range(slab_ref.shape[1])], axis=1)
        core = mm(slab, basis)
        core_ref[j] = low(core.T)
        inner = mm(low(core), rank_ref[...])
        sketch.append(jnp.sum(inner * weight, axis=0, keepdims=True))
    sketch = jnp.concatenate(sketch, axis=0)
    upper = low(sketch)
    lower = low(sketch - upper.astype(jnp.float32))
    copies = 64 // rows
    halves = jnp.concatenate([upper] * copies + [lower] * copies, axis=0)

    group = 256 // rows
    pairs = group // 2
    target = lax.broadcasted_iota(jnp.int32, (256, 256), 0)
    source = lax.broadcasted_iota(jnp.int32, (256, 256), 1)
    wanted = (target % rows) * group + 2 * ((target // rows) % pairs) + target // (rows * pairs)
    permute = low(jnp.where(source == wanted, 1.0, 0.0))
    full = planes // 128 * 128
    gap = jnp.zeros((128, 128 - 2 * (planes - full)), jnp.bfloat16)
    for g in range(rank // group):
        mixed = [core_ref[j, g * group : (g + 1) * group] for j in range(rows)]
        sorted_rows = low(mm(permute, jnp.concatenate(mixed, axis=0)))
        even, odd = sorted_rows[:128], sorted_rows[128:]
        split_ref[g * 128 : (g + 1) * 128] = jnp.concatenate(
            [even[:, :full], odd[:, :full], even[:, full:], odd[:, full:], gap, halves], axis=1
        )


def project(basis, sketch_plane, sketch_rank, moved):
    blocks, rows, planes, width = moved.shape
    rank = basis.shape[1]
    lanes = 2 * (planes // 128) * 128 + 128
    return pl.pallas_call(
        project_kernel,
        out_shape=jax.ShapeDtypeStruct((rank // 2 * rows, lanes + rank), jnp.bfloat16),
        in_specs=[VMEM] * 3 + [pl.BlockSpec(memory_space=pl.ANY)],
        out_specs=VMEM,
        scratch_shapes=[
            pltpu.VMEM((rows, rank, planes), jnp.bfloat16),
            pltpu.VMEM((rows, blocks, planes, width), jnp.bfloat16),
            pltpu.SemaphoreType.DMA((rows,)),
        ],
        compiler_params=PARAMS,
        cost_estimate=cost(2 * 10**9, 8 * 10**6),
        name="project",
    )(basis, sketch_plane, sketch_rank, moved)


def merge_kernel(got_ref, out_ref):
    blocks, count, _ = got_ref.shape
    planes = out_ref.shape[2]
    full = planes // 128 * 128
    rest = planes - full
    group = 256 // (2 * blocks)
    target = lax.broadcasted_iota(jnp.int32, (256, 256), 0)
    source = lax.broadcasted_iota(jnp.int32, (256, 256), 1)
    wanted = (target % (2 * blocks)) * group + target // (2 * blocks)
    permute = low(jnp.where(source == wanted, 1.0, 0.0))
    for g in range(count // group):
        rows = []
        for b in range(blocks):
            got = got_ref[b, g * group : (g + 1) * group]
            tail = 2 * full
            rows.append(jnp.concatenate([got[:, :full], got[:, tail : tail + rest]], axis=1))
            rows.append(
                jnp.concatenate([got[:, full:tail], got[:, tail + rest : tail + 2 * rest]], axis=1)
            )
        moved = mm(permute, jnp.concatenate(rows, axis=0))
        out_ref[g * group : (g + 1) * group] = moved.reshape(group, 2 * blocks, planes)


def merge(got, planes):
    return pl.pallas_call(
        merge_kernel,
        out_shape=jax.ShapeDtypeStruct((got.shape[1], 2 * got.shape[0], planes), jnp.float32),
        in_specs=[VMEM],
        out_specs=VMEM,
        compiler_params=PARAMS,
        cost_estimate=cost(10**8, 10**6),
        name="merge",
    )(got)


def exchange(blocks, axes):
    return lax.all_to_all(blocks, axes, split_axis=0, concat_axis=0, tiled=True)


def gather(rows, axes, count):
    shared = jnp.broadcast_to(rows[None], (count,) + rows.shape)
    return exchange(shared, axes).reshape(count * rows.shape[0], rows.shape[1])


def around(block, axes, step):
    count = lax.axis_size(axes)
    return lax.ppermute(block, axes, [(p, (p + step) % count) for p in range(count)])


def ordered(blocks, place):
    count = len(blocks)
    turned = jnp.stack(blocks[::-1] * 2)
    return lax.dynamic_slice_in_dim(turned, count - 1 - place, count, 0)


def collect(block, axes):
    count = lax.axis_size(axes)
    blocks = [block] + [around(block, axes, step) for step in range(1, count)]
    every = ordered(blocks, lax.axis_index(axes))
    return every.reshape((-1,) + block.shape[1:])


AF = ("z", "yh")
SA = ("x", "yl", "c")


def on_device(tensor, omega_two, omega_three, sketch_rank, sketch_plane):
    n_af = lax.axis_size(AF)
    n_sa = lax.axis_size(SA)
    n_all = n_af * n_sa
    local_rows, local_cols, planes = tensor.shape
    rank = omega_two.shape[1]
    fine_rows = local_rows // n_af

    rows = first_sums(tensor, omega_two, omega_three)
    some_rank = collect(sketch_rank, "yl")

    parts = exchange(rows.reshape(n_sa, -1, rank), SA)
    rows, some_rank = lax.optimization_barrier((jnp.sum(parts, axis=0), some_rank))
    rows = gather(rows, AF + ("yl",), n_af * 2)

    rows, tensor = lax.optimization_barrier((rows, tensor))
    pieces = jnp.swapaxes(tensor, 1, 2).reshape(n_af, fine_rows, planes, local_cols)
    moved = exchange(pieces, AF)

    rows = collect(collect(rows, "x"), "c")
    whole_rank = collect(collect(some_rank, "c"), "x").reshape(4, 2, 2, -1, rank)
    whole_rank = whole_rank.swapaxes(1, 2).reshape(rank, rank)
    basis_low = first_basis(rows)

    split = project(basis_low, sketch_plane, whole_rank, moved)
    got = exchange(split.reshape(n_all, fine_rows, -1), SA + AF).reshape(n_all * fine_rows, -1)
    core = second_core(got, around(got[:, -rank:], "c", 1))

    return merge(exchange(core.reshape(n_af, rank // n_af, -1), AF), planes)


def solution(mesh):
    grid = Mesh(mesh.devices.reshape(4, 2, 4, 2, 2), ("z", "yh", "x", "yl", "c"))
    placed = (P(SA, AF, None), P(SA, None), P(), P(SA, None), P())
    return jax.shard_map(
        on_device, mesh=grid, in_specs=placed, out_specs=P(AF, SA, None), check_vma=False
    )
```

```python
import jax
import jax.numpy as jnp
from jax import lax
from jax.experimental import pallas as pl
from jax.experimental.pallas import tpu as pltpu
from jax.sharding import Mesh
from jax.sharding import PartitionSpec as P

HIGH = lax.Precision.HIGHEST


NT = (((1,), (1,)), ((), ()))
NN = (((1,), (0,)), ((), ()))
TN = (((0,), (0,)), ((), ()))


def mm(a, b, dims=NN, precision=None):
    return lax.dot_general(a, b, dims, precision=precision, preferred_element_type=jnp.float32)


def low(x):
    return x.astype(jnp.bfloat16)


def halves_of(x):
    upper = low(x)
    return upper, low(x - upper.astype(jnp.float32))


def fine(a, b, dims=NN):
    return mm(a[0], b[0], dims) + (mm(a[0], b[1], dims) + mm(a[1], b[0], dims))


def inverse_factor(s, gram, basis_ref, a_ref, m_ref, turned):
    n = s.shape[1]
    row = lax.broadcasted_iota(jnp.int32, (n, n), 0)
    col = lax.broadcasted_iota(jnp.int32, (n, n), 1)
    eye = row == col
    one = jnp.where(eye, 1.0, 0.0)
    half = jnp.where(row > col, 1.0, 0.5 * one)

    sketch = halves_of(s)

    def put(inverse):
        inverse = halves_of(inverse)
        basis_ref[...] = low(fine(inverse, sketch, NT) if turned else fine(sketch, inverse, NT))

    on_diag = jnp.where(eye, gram, 0.0)
    inv_row = 0.9 * lax.rsqrt(jnp.sum(on_diag, axis=0, keepdims=True))
    inv_col = 0.9 * lax.rsqrt(jnp.sum(on_diag, axis=1, keepdims=True))
    scaled = gram * inv_col * inv_row

    h = scaled
    m = None
    early = 2
    for step in range(early):
        f = half * (h - one)
        fb = low(f)
        kb = low(one - f + half * mm(fb, fb, NT) + mm(fb, fb))
        m = kb if m is None else low(mm(kb, m))
        if step < early - 1:
            h = mm(low(mm(kb, low(h))), kb, NT)
    m = m.astype(jnp.float32)
    gram = halves_of(scaled)
    for _ in range(2):
        both = halves_of(m)
        r = fine(halves_of(fine(both, gram)), both, NT) - one
        m = m - fine(halves_of(half * r), both)
    good = jnp.logical_and(jnp.sum(r * r) < 1e-3, jnp.min(jnp.where(eye, m, 1.0)) > 0.0)
    put(m * inv_row)

    @pl.when(jnp.logical_not(good))
    def _():
        a_ref[...] = scaled
        m_ref[...] = one

        def step(j, carry):
            a = a_ref[...]
            pivot_row = a_ref[pl.ds(j, 1), :]
            unit_row = m_ref[pl.ds(j, 1), :]
            column = jnp.sum(jnp.where(col == j, a, 0.0), axis=1, keepdims=True)
            pivot = jnp.sum(jnp.where(col[:1] == j, pivot_row, 0.0), axis=1, keepdims=True)
            f = jnp.where(row[:, :1] > j, column / pivot, 0.0)
            a_ref[...] = a - f * pivot_row
            m_ref[...] = m_ref[...] - f * unit_row
            return carry

        lax.fori_loop(0, n, step, 0)
        pivots = jnp.sum(jnp.where(eye, a_ref[...], 0.0), axis=1, keepdims=True)
        direct = m_ref[...] * lax.rsqrt(pivots) * inv_row
        put(direct)


VMEM = pl.BlockSpec(memory_space=pltpu.VMEM)
PARAMS = pltpu.CompilerParams(vmem_limit_bytes=32 * 1024 * 1024)
ROOMY = pltpu.CompilerParams(vmem_limit_bytes=60 * 1024 * 1024)


def cost(flops, size):
    return pl.CostEstimate(flops=flops, bytes_accessed=size, transcendentals=0)


def first_basis_kernel(s_ref, basis_ref, a_ref, m_ref):
    places = [
        (((c * 4 + x) * 4 + z) * 2 + yh) * 2 + yl
        for z in range(4)
        for yh in range(2)
        for x in range(4)
        for yl in range(2)
        for c in range(2)
    ]
    s = jnp.concatenate([s_ref[place * 8 : place * 8 + 8] for place in places], axis=0)
    inverse_factor(s, mm(s, s, TN, HIGH), basis_ref, a_ref, m_ref, False)


def first_basis(sketch):
    n = sketch.shape[1]
    return pl.pallas_call(
        first_basis_kernel,
        out_shape=jax.ShapeDtypeStruct(sketch.shape, jnp.bfloat16),
        in_specs=[VMEM],
        out_specs=VMEM,
        scratch_shapes=[pltpu.VMEM((n, n), jnp.float32)] * 2,
        compiler_params=PARAMS,
        cost_estimate=cost(0, 0),
        name="first_basis",
    )(sketch)


def second_core_kernel(got_ref, other_ref, core_ref, basis_ref, a_ref, m_ref):
    lanes = core_ref.shape[1]
    here, there = got_ref[:, lanes:], other_ref[...]
    sketch = here.astype(jnp.float32) + there.astype(jnp.float32)
    cross = mm(here, there, TN)
    gram = mm(here, here, TN) + (cross + cross.T) + mm(there, there, TN)
    inverse_factor(sketch, gram, basis_ref, a_ref, m_ref, True)
    core_ref[...] = mm(basis_ref[...], got_ref[:, :lanes]).astype(core_ref.dtype)


def second_core(got, other):
    n = other.shape[1]
    lanes = got.shape[1] - n
    return pl.pallas_call(
        second_core_kernel,
        out_shape=jax.ShapeDtypeStruct((n, lanes), jnp.bfloat16),
        in_specs=[VMEM] * 2,
        out_specs=VMEM,
        scratch_shapes=[pltpu.VMEM((n, got.shape[0]), jnp.bfloat16)]
        + [pltpu.VMEM((n, n), jnp.float32)] * 2,
        compiler_params=PARAMS,
        cost_estimate=cost(4 * 10**9, 3 * 10**6),
        name="second_core",
    )(got, other)


def first_sums_kernel(two_ref, three_ref, slabs_ref, out_ref):
    step = pl.program_id(0)
    count = slabs_ref.shape[0]
    weight = two_ref[pl.ds(pl.multiple_of(step * count, count), count), :]
    weight = weight.astype(jnp.float32)
    total = None
    for j in range(count):
        inner = mm(slabs_ref[j], three_ref[...], TN)
        term = inner * weight[j : j + 1]
        total = term if total is None else total + term

    @pl.when(step == 0)
    def _():
        out_ref[...] = total

    @pl.when(step > 0)
    def _():
        out_ref[...] += total


def first_sums(tensor, omega_two, omega_three):
    rows, cols, planes = tensor.shape
    rank = omega_two.shape[1]
    count = 32
    return pl.pallas_call(
        first_sums_kernel,
        grid=(rows // count,),
        out_shape=jax.ShapeDtypeStruct((cols, rank), jnp.float32),
        in_specs=[
            pl.BlockSpec((rows, rank), lambda step: (0, 0)),
            pl.BlockSpec((planes, rank), lambda step: (0, 0)),
            pl.BlockSpec((count, planes, cols), lambda step: (step, 0, 0)),
        ],
        out_specs=pl.BlockSpec((cols, rank), lambda step: (0, 0)),
        compiler_params=ROOMY,
        cost_estimate=cost(10**9, 5 * 10**6),
        name="first_sums",
    )(omega_two, omega_three, jnp.swapaxes(tensor, 1, 2))


def project_kernel(basis_ref, plane_ref, rank_ref, moved_ref, split_ref, core_ref, slab_ref, sems):
    rows, rank, planes = core_ref.shape
    loads = [
        pltpu.make_async_copy(moved_ref.at[:, j], slab_ref.at[j], sems.at[j]) for j in range(rows)
    ]
    for load in loads:
        load.start()
    basis = basis_ref[...]
    weight = plane_ref[...].astype(jnp.float32)
    sketch = []
    batch = 4
    for first in range(0, rows, batch):
        slabs = []
        for j in range(first, first + batch):
            loads[j].wait()
            slabs.append(jnp.concatenate([slab_ref[j, b] for b in range(slab_ref.shape[1])], axis=1))
        cores = mm(jnp.concatenate(slabs, axis=0), basis)
        inners = mm(low(cores), rank_ref[...])
        for at in range(batch):
            here = slice(at * planes, (at + 1) * planes)
            core_ref[first + at] = low(cores[here].T)
            sketch.append(jnp.sum(inners[here] * weight, axis=0, keepdims=True))
    sketch = jnp.concatenate(sketch, axis=0)
    upper = low(sketch)
    lower = low(sketch - upper.astype(jnp.float32))
    copies = 64 // rows
    halves = jnp.concatenate([upper] * copies + [lower] * copies, axis=0)

    group = 256 // rows
    pairs = group // 2
    target = lax.broadcasted_iota(jnp.int32, (256, 256), 0)
    source = lax.broadcasted_iota(jnp.int32, (256, 256), 1)
    wanted = (target % rows) * group + 2 * ((target // rows) % pairs) + target // (rows * pairs)
    permute = low(jnp.where(source == wanted, 1.0, 0.0))
    full = planes // 128 * 128
    gap = jnp.zeros((128, 128 - 2 * (planes - full)), jnp.bfloat16)
    for g in range(rank // group):
        mixed = [core_ref[j, g * group : (g + 1) * group] for j in range(rows)]
        sorted_rows = low(mm(permute, jnp.concatenate(mixed, axis=0)))
        even, odd = sorted_rows[:128], sorted_rows[128:]
        split_ref[g * 128 : (g + 1) * 128] = jnp.concatenate(
            [even[:, :full], odd[:, :full], even[:, full:], odd[:, full:], gap, halves], axis=1
        )


def project(basis, sketch_plane, sketch_rank, moved):
    blocks, rows, planes, width = moved.shape
    rank = basis.shape[1]
    lanes = 2 * (planes // 128) * 128 + 128
    return pl.pallas_call(
        project_kernel,
        out_shape=jax.ShapeDtypeStruct((rank // 2 * rows, lanes + rank), jnp.bfloat16),
        in_specs=[VMEM] * 3 + [pl.BlockSpec(memory_space=pl.ANY)],
        out_specs=VMEM,
        scratch_shapes=[
            pltpu.VMEM((rows, rank, planes), jnp.bfloat16),
            pltpu.VMEM((rows, blocks, planes, width), jnp.bfloat16),
            pltpu.SemaphoreType.DMA((rows,)),
        ],
        compiler_params=PARAMS,
        cost_estimate=cost(2 * 10**9, 8 * 10**6),
        name="project",
    )(basis, sketch_plane, sketch_rank, moved)


def merge_kernel(got_ref, out_ref):
    blocks, count, _ = got_ref.shape
    planes = out_ref.shape[2]
    full = planes // 128 * 128
    rest = planes - full
    group = 256 // (2 * blocks)
    target = lax.broadcasted_iota(jnp.int32, (256, 256), 0)
    source = lax.broadcasted_iota(jnp.int32, (256, 256), 1)
    wanted = (target % (2 * blocks)) * group + target // (2 * blocks)
    permute = low(jnp.where(source == wanted, 1.0, 0.0))
    for g in range(count // group):
        rows = []
        for b in range(blocks):
            got = got_ref[b, g * group : (g + 1) * group]
            tail = 2 * full
            rows.append(jnp.concatenate([got[:, :full], got[:, tail : tail + rest]], axis=1))
            rows.append(
                jnp.concatenate([got[:, full:tail], got[:, tail + rest : tail + 2 * rest]], axis=1)
            )
        moved = mm(permute, jnp.concatenate(rows, axis=0))
        out_ref[g * group : (g + 1) * group] = moved.reshape(group, 2 * blocks, planes)


def merge(got, planes):
    return pl.pallas_call(
        merge_kernel,
        out_shape=jax.ShapeDtypeStruct((got.shape[1], 2 * got.shape[0], planes), jnp.float32),
        in_specs=[VMEM],
        out_specs=VMEM,
        compiler_params=PARAMS,
        cost_estimate=cost(10**8, 10**6),
        name="merge",
    )(got)


def exchange(blocks, axes):
    return lax.all_to_all(blocks, axes, split_axis=0, concat_axis=0, tiled=True)


def gather(rows, axes, count):
    shared = jnp.broadcast_to(rows[None], (count,) + rows.shape)
    return exchange(shared, axes).reshape(count * rows.shape[0], rows.shape[1])


def around(block, axes, step):
    count = lax.axis_size(axes)
    return lax.ppermute(block, axes, [(p, (p + step) % count) for p in range(count)])


def ordered(blocks, place):
    count = len(blocks)
    turned = jnp.stack(blocks[::-1] * 2)
    return lax.dynamic_slice_in_dim(turned, count - 1 - place, count, 0)


def collect(block, axes):
    count = lax.axis_size(axes)
    blocks = [block] + [around(block, axes, step) for step in range(1, count)]
    every = ordered(blocks, lax.axis_index(axes))
    return every.reshape((-1,) + block.shape[1:])


AF = ("z", "yh")
SA = ("x", "yl", "c")


def on_device(tensor, omega_two, omega_three, sketch_rank, sketch_plane):
    n_af = lax.axis_size(AF)
    n_sa = lax.axis_size(SA)
    n_all = n_af * n_sa
    local_rows, local_cols, planes = tensor.shape
    rank = omega_two.shape[1]
    fine_rows = local_rows // n_af

    rows = first_sums(tensor, omega_two, omega_three)
    some_rank = collect(sketch_rank, "yl")

    parts = exchange(rows.reshape(n_sa, -1, rank), SA)
    rows, some_rank = lax.optimization_barrier((jnp.sum(parts, axis=0), some_rank))
    rows = gather(rows, AF + ("yl",), n_af * 2)

    rows, tensor = lax.optimization_barrier((rows, tensor))
    pieces = jnp.swapaxes(tensor, 1, 2).reshape(n_af, fine_rows, planes, local_cols)
    moved = exchange(pieces, AF)

    rows = collect(collect(rows, "x"), "c")
    whole_rank = collect(collect(some_rank, "c"), "x").reshape(4, 2, 2, -1, rank)
    whole_rank = whole_rank.swapaxes(1, 2).reshape(rank, rank)
    basis_low = first_basis(rows)

    split = project(basis_low, sketch_plane, whole_rank, moved)
    got = exchange(split.reshape(n_all, fine_rows, -1), SA + AF).reshape(n_all * fine_rows, -1)
    core = second_core(got, around(got[:, -rank:], "c", 1))

    return merge(exchange(core.reshape(n_af, rank // n_af, -1), AF), planes)


def solution(mesh):
    grid = Mesh(mesh.devices.reshape(4, 2, 4, 2, 2), ("z", "yh", "x", "yl", "c"))
    placed = (P(SA, AF, None), P(SA, None), P(), P(SA, None), P())
    return jax.shard_map(
        on_device, mesh=grid, in_specs=placed, out_specs=P(AF, SA, None), check_vma=False
    )
```

```python
import jax
import jax.numpy as jnp
from jax import lax
from jax.experimental import pallas as pl
from jax.experimental.pallas import tpu as pltpu
from jax.sharding import Mesh
from jax.sharding import PartitionSpec as P

HIGH = lax.Precision.HIGHEST


NT = (((1,), (1,)), ((), ()))
NN = (((1,), (0,)), ((), ()))
TN = (((0,), (0,)), ((), ()))


def mm(a, b, dims=NN, precision=None):
    return lax.dot_general(a, b, dims, precision=precision, preferred_element_type=jnp.float32)


def low(x):
    return x.astype(jnp.bfloat16)


def halves_of(x):
    upper = low(x)
    return upper, low(x - upper.astype(jnp.float32))


def fine(a, b, dims=NN):
    return mm(a[0], b[0], dims) + (mm(a[0], b[1], dims) + mm(a[1], b[0], dims))


def inverse_factor(s, gram, basis_ref, a_ref, m_ref, turned):
    n = s.shape[1]
    row = lax.broadcasted_iota(jnp.int32, (n, n), 0)
    col = lax.broadcasted_iota(jnp.int32, (n, n), 1)
    eye = row == col
    one = jnp.where(eye, 1.0, 0.0)
    half = jnp.where(row > col, 1.0, 0.5 * one)

    sketch = halves_of(s)

    def put(inverse):
        inverse = halves_of(inverse)
        basis_ref[...] = low(fine(inverse, sketch, NT) if turned else fine(sketch, inverse, NT))

    on_diag = jnp.where(eye, gram, 0.0)
    inv_row = 0.9 * lax.rsqrt(jnp.sum(on_diag, axis=0, keepdims=True))
    inv_col = 0.9 * lax.rsqrt(jnp.sum(on_diag, axis=1, keepdims=True))
    scaled = gram * inv_col * inv_row

    h = scaled
    m = None
    early = 2
    for step in range(early):
        f = half * (h - one)
        fb = low(f)
        kb = low(one - f + half * mm(fb, fb, NT) + mm(fb, fb))
        m = kb if m is None else low(mm(kb, m))
        if step < early - 1:
            h = mm(low(mm(kb, low(h))), kb, NT)
    m = m.astype(jnp.float32)
    gram = halves_of(scaled)
    for _ in range(2):
        both = halves_of(m)
        r = fine(halves_of(fine(both, gram)), both, NT) - one
        m = m - fine(halves_of(half * r), both)
    good = jnp.logical_and(jnp.sum(r * r) < 1e-3, jnp.min(jnp.where(eye, m, 1.0)) > 0.0)
    put(m * inv_row)

    @pl.when(jnp.logical_not(good))
    def _():
        a_ref[...] = scaled
        m_ref[...] = one

        def step(j, carry):
            a = a_ref[...]
            pivot_row = a_ref[pl.ds(j, 1), :]
            unit_row = m_ref[pl.ds(j, 1), :]
            column = jnp.sum(jnp.where(col == j, a, 0.0), axis=1, keepdims=True)
            pivot = jnp.sum(jnp.where(col[:1] == j, pivot_row, 0.0), axis=1, keepdims=True)
            f = jnp.where(row[:, :1] > j, column / pivot, 0.0)
            a_ref[...] = a - f * pivot_row
            m_ref[...] = m_ref[...] - f * unit_row
            return carry

        lax.fori_loop(0, n, step, 0)
        pivots = jnp.sum(jnp.where(eye, a_ref[...], 0.0), axis=1, keepdims=True)
        direct = m_ref[...] * lax.rsqrt(pivots) * inv_row
        put(direct)


VMEM = pl.BlockSpec(memory_space=pltpu.VMEM)
PARAMS = pltpu.CompilerParams(vmem_limit_bytes=32 * 1024 * 1024)
ROOMY = pltpu.CompilerParams(vmem_limit_bytes=60 * 1024 * 1024)


def cost(flops, size):
    return pl.CostEstimate(flops=flops, bytes_accessed=size, transcendentals=0)


def first_basis_kernel(s_ref, basis_ref, a_ref, m_ref):
    places = [
        (((c * 4 + x) * 4 + z) * 2 + yh) * 2 + yl
        for z in range(4)
        for yh in range(2)
        for x in range(4)
        for yl in range(2)
        for c in range(2)
    ]
    s = jnp.concatenate([s_ref[place * 8 : place * 8 + 8] for place in places], axis=0)
    inverse_factor(s, mm(s, s, TN, HIGH), basis_ref, a_ref, m_ref, False)


def first_basis(sketch):
    n = sketch.shape[1]
    return pl.pallas_call(
        first_basis_kernel,
        out_shape=jax.ShapeDtypeStruct(sketch.shape, jnp.bfloat16),
        in_specs=[VMEM],
        out_specs=VMEM,
        scratch_shapes=[pltpu.VMEM((n, n), jnp.float32)] * 2,
        compiler_params=PARAMS,
        cost_estimate=cost(0, 0),
        name="first_basis",
    )(sketch)


def second_core_kernel(got_ref, other_ref, core_ref, basis_ref, a_ref, m_ref):
    lanes = core_ref.shape[1]
    here, there = got_ref[:, lanes:], other_ref[...]
    sketch = here.astype(jnp.float32) + there.astype(jnp.float32)
    cross = mm(here, there, TN)
    gram = mm(here, here, TN) + (cross + cross.T) + mm(there, there, TN)
    inverse_factor(sketch, gram, basis_ref, a_ref, m_ref, True)
    core_ref[...] = mm(basis_ref[...], got_ref[:, :lanes]).astype(core_ref.dtype)


def second_core(got, other):
    n = other.shape[1]
    lanes = got.shape[1] - n
    return pl.pallas_call(
        second_core_kernel,
        out_shape=jax.ShapeDtypeStruct((n, lanes), jnp.bfloat16),
        in_specs=[VMEM] * 2,
        out_specs=VMEM,
        scratch_shapes=[pltpu.VMEM((n, got.shape[0]), jnp.bfloat16)]
        + [pltpu.VMEM((n, n), jnp.float32)] * 2,
        compiler_params=PARAMS,
        cost_estimate=cost(4 * 10**9, 3 * 10**6),
        name="second_core",
    )(got, other)


def first_sums_kernel(two_ref, three_ref, slabs_ref, out_ref):
    step = pl.program_id(0)
    count = slabs_ref.shape[0]
    weight = two_ref[pl.ds(pl.multiple_of(step * count, count), count), :]
    weight = weight.astype(jnp.float32)
    total = None
    batch = 4
    cols = slabs_ref.shape[2]
    for first in range(0, count, batch):
        slabs = jnp.concatenate([slabs_ref[first + at] for at in range(batch)], axis=1)
        inner = mm(slabs, three_ref[...], TN)
        for at in range(batch):
            j = first + at
            term = inner[at * cols : (at + 1) * cols] * weight[j : j + 1]
            total = term if total is None else total + term

    @pl.when(step == 0)
    def _():
        out_ref[...] = total

    @pl.when(step > 0)
    def _():
        out_ref[...] += total


def first_sums(tensor, omega_two, omega_three):
    rows, cols, planes = tensor.shape
    rank = omega_two.shape[1]
    count = 32
    return pl.pallas_call(
        first_sums_kernel,
        grid=(rows // count,),
        out_shape=jax.ShapeDtypeStruct((cols, rank), jnp.float32),
        in_specs=[
            pl.BlockSpec((rows, rank), lambda step: (0, 0)),
            pl.BlockSpec((planes, rank), lambda step: (0, 0)),
            pl.BlockSpec((count, planes, cols), lambda step: (step, 0, 0)),
        ],
        out_specs=pl.BlockSpec((cols, rank), lambda step: (0, 0)),
        compiler_params=ROOMY,
        cost_estimate=cost(10**9, 5 * 10**6),
        name="first_sums",
    )(omega_two, omega_three, jnp.swapaxes(tensor, 1, 2))


def project_kernel(basis_ref, plane_ref, rank_ref, moved_ref, split_ref, core_ref, slab_ref, sems):
    rows, rank, planes = core_ref.shape
    loads = [
        pltpu.make_async_copy(moved_ref.at[:, j], slab_ref.at[j], sems.at[j]) for j in range(rows)
    ]
    for load in loads:
        load.start()
    basis = basis_ref[...]
    weight = plane_ref[...].astype(jnp.float32)
    sketch = []
    batch = 2
    for first in range(0, rows, batch):
        slabs = []
        for j in range(first, first + batch):
            loads[j].wait()
            slabs.append(jnp.concatenate([slab_ref[j, b] for b in range(slab_ref.shape[1])], axis=1))
        cores = mm(jnp.concatenate(slabs, axis=0), basis)
        inners = mm(low(cores), rank_ref[...])
        for at in range(batch):
            here = slice(at * planes, (at + 1) * planes)
            core_ref[first + at] = low(cores[here].T)
            sketch.append(jnp.sum(inners[here] * weight, axis=0, keepdims=True))
    sketch = jnp.concatenate(sketch, axis=0)
    upper = low(sketch)
    lower = low(sketch - upper.astype(jnp.float32))
    copies = 64 // rows
    halves = jnp.concatenate([upper] * copies + [lower] * copies, axis=0)

    group = 256 // rows
    pairs = group // 2
    target = lax.broadcasted_iota(jnp.int32, (256, 256), 0)
    source = lax.broadcasted_iota(jnp.int32, (256, 256), 1)
    wanted = (target % rows) * group + 2 * ((target // rows) % pairs) + target // (rows * pairs)
    permute = low(jnp.where(source == wanted, 1.0, 0.0))
    full = planes // 128 * 128
    gap = jnp.zeros((128, 128 - 2 * (planes - full)), jnp.bfloat16)
    for g in range(rank // group):
        mixed = [core_ref[j, g * group : (g + 1) * group] for j in range(rows)]
        sorted_rows = low(mm(permute, jnp.concatenate(mixed, axis=0)))
        even, odd = sorted_rows[:128], sorted_rows[128:]
        split_ref[g * 128 : (g + 1) * 128] = jnp.concatenate(
            [even[:, :full], odd[:, :full], even[:, full:], odd[:, full:], gap, halves], axis=1
        )


def project(basis, sketch_plane, sketch_rank, moved):
    blocks, rows, planes, width = moved.shape
    rank = basis.shape[1]
    lanes = 2 * (planes // 128) * 128 + 128
    return pl.pallas_call(
        project_kernel,
        out_shape=jax.ShapeDtypeStruct((rank // 2 * rows, lanes + rank), jnp.bfloat16),
        in_specs=[VMEM] * 3 + [pl.BlockSpec(memory_space=pl.ANY)],
        out_specs=VMEM,
        scratch_shapes=[
            pltpu.VMEM((rows, rank, planes), jnp.bfloat16),
            pltpu.VMEM((rows, blocks, planes, width), jnp.bfloat16),
            pltpu.SemaphoreType.DMA((rows,)),
        ],
        compiler_params=PARAMS,
        cost_estimate=cost(2 * 10**9, 8 * 10**6),
        name="project",
    )(basis, sketch_plane, sketch_rank, moved)


def merge_kernel(got_ref, out_ref):
    blocks, count, _ = got_ref.shape
    planes = out_ref.shape[2]
    full = planes // 128 * 128
    rest = planes - full
    group = 256 // (2 * blocks)
    target = lax.broadcasted_iota(jnp.int32, (256, 256), 0)
    source = lax.broadcasted_iota(jnp.int32, (256, 256), 1)
    wanted = (target % (2 * blocks)) * group + target // (2 * blocks)
    permute = low(jnp.where(source == wanted, 1.0, 0.0))
    for g in range(count // group):
        rows = []
        for b in range(blocks):
            got = got_ref[b, g * group : (g + 1) * group]
            tail = 2 * full
            rows.append(jnp.concatenate([got[:, :full], got[:, tail : tail + rest]], axis=1))
            rows.append(
                jnp.concatenate([got[:, full:tail], got[:, tail + rest : tail + 2 * rest]], axis=1)
            )
        moved = mm(permute, jnp.concatenate(rows, axis=0))
        out_ref[g * group : (g + 1) * group] = moved.reshape(group, 2 * blocks, planes)


def merge(got, planes):
    return pl.pallas_call(
        merge_kernel,
        out_shape=jax.ShapeDtypeStruct((got.shape[1], 2 * got.shape[0], planes), jnp.float32),
        in_specs=[VMEM],
        out_specs=VMEM,
        compiler_params=PARAMS,
        cost_estimate=cost(10**8, 10**6),
        name="merge",
    )(got)


def exchange(blocks, axes):
    return lax.all_to_all(blocks, axes, split_axis=0, concat_axis=0, tiled=True)


def gather(rows, axes, count):
    shared = jnp.broadcast_to(rows[None], (count,) + rows.shape)
    return exchange(shared, axes).reshape(count * rows.shape[0], rows.shape[1])


def around(block, axes, step):
    count = lax.axis_size(axes)
    return lax.ppermute(block, axes, [(p, (p + step) % count) for p in range(count)])


def ordered(blocks, place):
    count = len(blocks)
    turned = jnp.stack(blocks[::-1] * 2)
    return lax.dynamic_slice_in_dim(turned, count - 1 - place, count, 0)


def collect(block, axes):
    count = lax.axis_size(axes)
    blocks = [block] + [around(block, axes, step) for step in range(1, count)]
    every = ordered(blocks, lax.axis_index(axes))
    return every.reshape((-1,) + block.shape[1:])


AF = ("z", "yh")
SA = ("x", "yl", "c")


def on_device(tensor, omega_two, omega_three, sketch_rank, sketch_plane):
    n_af = lax.axis_size(AF)
    n_sa = lax.axis_size(SA)
    n_all = n_af * n_sa
    local_rows, local_cols, planes = tensor.shape
    rank = omega_two.shape[1]
    fine_rows = local_rows // n_af

    rows = first_sums(tensor, omega_two, omega_three)
    some_rank = collect(sketch_rank, "yl")

    parts = exchange(rows.reshape(n_sa, -1, rank), SA)
    rows, some_rank = lax.optimization_barrier((jnp.sum(parts, axis=0), some_rank))
    rows = gather(rows, AF + ("yl",), n_af * 2)

    rows, tensor = lax.optimization_barrier((rows, tensor))
    pieces = jnp.swapaxes(tensor, 1, 2).reshape(n_af, fine_rows, planes, local_cols)
    moved = exchange(pieces, AF)

    rows = collect(collect(rows, "x"), "c")
    whole_rank = collect(collect(some_rank, "c"), "x").reshape(4, 2, 2, -1, rank)
    whole_rank = whole_rank.swapaxes(1, 2).reshape(rank, rank)
    basis_low = first_basis(rows)

    split = project(basis_low, sketch_plane, whole_rank, moved)
    got = exchange(split.reshape(n_all, fine_rows, -1), SA + AF).reshape(n_all * fine_rows, -1)
    core = second_core(got, around(got[:, -rank:], "c", 1))

    return merge(exchange(core.reshape(n_af, rank // n_af, -1), AF), planes)


def solution(mesh):
    grid = Mesh(mesh.devices.reshape(4, 2, 4, 2, 2), ("z", "yh", "x", "yl", "c"))
    placed = (P(SA, AF, None), P(SA, None), P(), P(SA, None), P())
    return jax.shard_map(
        on_device, mesh=grid, in_specs=placed, out_specs=P(AF, SA, None), check_vma=False
    )
```
